32 devices in a mesh: grp: 2 (over x), qa: 16 (over z, y, core).
Axes of the slice: x: 2, y: 2, z: 4, core: 2. Of those that a mesh axis runs over, the one named last changes fastest.
Arguments:
- state: float32 [2, 2097152], P(None, ('grp', 'qa')), parts along dimension 1, may hold values from -6 to 6
- adjoint: float32 [2, 2097152], P(None, ('grp', 'qa')), parts along dimension 1, may hold values from -6 to 6
- gates: float32 [8, 3, 2, 128, 128], P('grp'), parts along dimension 0, may hold values from -0.375 to 0.375
Outputs:
- state_start: float32 [2, 2097152], P(None, ('grp', 'qa')), parts along dimension 1
- adjoint_start: float32 [2, 2097152], P(None, ('grp', 'qa')), parts along dimension 1
- grads: float32 [8, 3, 2, 128, 128], P('grp'), parts along dimension 0
The draws below stay inside these ranges and needn't reach their ends.
There are 2 independent parts, one for each index of `grp`. The reference program is written for one: setup_inputs(seed, part) draws one part's arguments, and reference() takes and returns one part's arrays. A program takes and returns all parts, laid end to end along the dimension named above; each array names one. Nothing has to cross between parts.
All inputs are finite; a program needn't handle non-finite values.
Results may differ from the reference program's by a relative error of at most 0.00014.
Values sent between devices are 32-bit elements; how exact they have to be, the bound alone decides.
No kernel may reach another device: no remote copies, remote signals or barrier semaphores. Data moves between devices by JAX's collectives and lax.ppermute only.
A program may use at most 64 MiB of HBM per device.

```python
import math
import jax
import jax.numpy as jnp
from jax import lax

GATE = 128
CB = 4
ROUNDS = 4
AMPS = 1048576
N_QA = 16


def level_of(key, dims, pieces, smallest, high):
    level = 1.0
    for axis_at, blocks in pieces:
        heights = jax.random.uniform(jax.random.fold_in(jax.random.fold_in(key, 6), axis_at), (blocks,), jnp.float32, smallest / len(pieces), high / len(pieces))
        level = level * jnp.repeat(jnp.exp(heights), dims[axis_at] // blocks).reshape((-1,) + (1,) * (len(dims) - 1 - axis_at))
    return level


def bell_draw(own_key, extent, spread, reach, pieces=(), held_as=jnp.bfloat16):
    drawn = jax.random.normal(own_key, extent, jnp.float32) * spread
    if len(pieces) > 0:
        drawn = level_of(own_key, extent, pieces, -0.22, 0.18) * drawn
    return jnp.clip(drawn, min=-reach, max=reach).astype(held_as)


def setup_inputs(seed: int = 0, part: int = 0) -> dict:
    key_list = jax.random.split(jax.random.key(seed), 4)
    own_keys = jax.random.split(jax.random.fold_in(key_list[3], part), 4)
    return {
        "state": bell_draw(own_keys[0], (2, AMPS), 1.0, 6.0, ((1, 16),), jnp.float32),
        "adjoint": bell_draw(own_keys[1], (2, AMPS), 1.0, 6.0, ((1, 16),), jnp.float32),
        "gates": bell_draw(own_keys[2], (ROUNDS, 3, 2, GATE, GATE), (2 * GATE) ** -0.5, 0.375, (), jnp.float32),
    }


HIGHEST = lax.Precision.HIGHEST

def undo_left(real_gate, imag_gate, amplitudes):

    def product(matrix, values):
        return jnp.einsum('ji,pjq->piq', matrix, values, precision=HIGHEST)
    return jnp.stack([product(real_gate, amplitudes[0]) + product(imag_gate, amplitudes[1]), product(real_gate, amplitudes[1]) - product(imag_gate, amplitudes[0])])

def undo_right(real_gate, imag_gate, amplitudes):

    def product(matrix, values):
        return jnp.dot(values, matrix, precision=HIGHEST)
    return jnp.stack([product(real_gate, amplitudes[0]) + product(imag_gate, amplitudes[1]), product(real_gate, amplitudes[1]) - product(imag_gate, amplitudes[0])])

def outer_left(adjoint_part, state_part):

    def contract(first, second):
        return jnp.einsum('piq,pjq->ij', first, second, precision=HIGHEST)
    real_part = contract(adjoint_part[0], state_part[0]) + contract(adjoint_part[1], state_part[1])
    imag_part = contract(adjoint_part[1], state_part[0]) - contract(adjoint_part[0], state_part[1])
    return jnp.stack([real_part, imag_part])

def outer_right(adjoint_part, state_part):

    def contract(first, second):
        return jnp.einsum('pi,pj->ij', first, second, precision=HIGHEST)
    real_part = contract(adjoint_part[0], state_part[0]) + contract(adjoint_part[1], state_part[1])
    imag_part = contract(adjoint_part[1], state_part[0]) - contract(adjoint_part[0], state_part[1])
    return jnp.stack([real_part, imag_part])

def reference(state, adjoint, gates):
    shards = N_QA
    local_size = GATE * CB * GATE
    factor = 1.0 / math.sqrt(shards * CB * GATE)

    def exchanged(amplitudes):
        return amplitudes.reshape(2, shards, shards, local_size // shards).swapaxes(1, 2).reshape(2, shards * local_size)
    state_now = state
    adjoint_now = adjoint
    results = []
    for number in reversed(range(ROUNDS)):
        state_now = exchanged(state_now)
        adjoint_now = exchanged(adjoint_now)
        round_grads = [None, None, None]
        for position in (2, 1, 0):
            real_gate = gates[number, position, 0]
            imag_gate = gates[number, position, 1]
            if position == 1:
                layout = (2, shards * local_size // GATE, GATE)
                undoing = undo_right
                pairing = outer_right
            elif position == 0:
                layout = (2, shards, GATE, CB * GATE)
                undoing = undo_left
                pairing = outer_left
            else:
                layout = (2, shards * CB, GATE, GATE)
                undoing = undo_left
                pairing = outer_left
            before = undoing(real_gate, imag_gate, state_now.reshape(layout))
            round_grads[position] = factor * pairing(adjoint_now.reshape(layout), before)
            adjoint_now = undoing(real_gate, imag_gate, adjoint_now.reshape(layout)).reshape(2, shards * local_size)
            state_now = before.reshape(2, shards * local_size)
        results.append(jnp.stack(round_grads))
    grads = jnp.stack(results[::-1])
    return (state_now, adjoint_now, grads)
```

```python
import functools
import math

import jax
import jax.numpy as jnp
from jax import lax
from jax.experimental import pallas as pl
from jax.experimental.pallas import tpu as pltpu
from jax.sharding import PartitionSpec as P

TILE = 8
VMEM = pl.BlockSpec(memory_space=pltpu.VMEM)
SMEM = pl.BlockSpec(memory_space=pltpu.SMEM)
F32 = jnp.float32
BF16 = jnp.bfloat16


def call(body, out_shape, operands, flops, in_specs=None, scratch=(), limit=24 << 20):
    outs = jax.tree.leaves(out_shape)
    moved = sum(math.prod(a.shape) * a.dtype.itemsize for a in (*operands, *outs))
    return pl.pallas_call(
        body,
        out_shape=out_shape,
        in_specs=in_specs or [VMEM] * len(operands),
        out_specs=jax.tree.map(lambda _: VMEM, out_shape),
        scratch_shapes=scratch,
        compiler_params=pltpu.CompilerParams(vmem_limit_bytes=limit),
        cost_estimate=pl.CostEstimate(flops=flops, bytes_accessed=moved, transcendentals=0),
    )(*operands)


def halves(x):
    high = x.astype(BF16)
    return high, (x - high.astype(F32)).astype(BF16)


def contract(first, second, dims):
    dot = functools.partial(
        lax.dot_general, dimension_numbers=(dims, ((), ())), preferred_element_type=F32
    )
    return dot(first[0], second[0]) + (dot(first[0], second[1]) + dot(first[1], second[0]))


def left(matrix, x):
    return contract((matrix[0], matrix[1]), halves(x), ((1,), (0,)))


def right(x, matrix):
    return contract(halves(x), (matrix[0], matrix[1]), ((1,), (0,)))


def order(gate, blocks):
    rows = lax.broadcasted_iota(jnp.int32, (gate, gate), 0)
    columns = lax.broadcasted_iota(jnp.int32, (gate, gate), 1)
    inside = columns % TILE
    middle = (columns // TILE) % blocks
    tile = columns // (TILE * blocks)
    return (rows == (tile * TILE + inside) * blocks + middle).astype(F32)


def exact(first, second, dims):
    return lax.dot_general(
        first, second, (dims, ((), ())), precision=lax.Precision.HIGHEST, preferred_element_type=F32
    )


def prepare_body(rounds, gate, blocks, gates_ref, out_ref):
    permutation = order(gate, blocks)
    for number in range(rounds):
        for position in range(3):
            real = gates_ref[number, position, 0]
            imag = gates_ref[number, position, 1]
            if position == 2:
                real, imag = (
                    exact(exact(permutation, u, ((0,), (0,))), permutation, ((1,), (0,))) for u in (real, imag)
                )
            if position == 1:
                quarters = ((real, -imag), (imag, real))
            else:
                real, imag = real.T, imag.T
                quarters = ((real, imag), (-imag, real))
            for i in range(2):
                for j in range(2):
                    for half, value in enumerate(halves(quarters[i][j])):
                        out_ref[number, position, half, pl.ds(i * gate, gate), pl.ds(j * gate, gate)] = value


def enter_body(gate, blocks, state_ref, adjoint_ref, out_ref):
    for array, ref in enumerate((state_ref, adjoint_ref)):
        for part in range(2):
            for c in range(blocks):
                rows = ref[pl.ds(c * 2 + part, gate, stride=2 * blocks), :]
                at = ((array * 2 + part) * blocks + c) * TILE
                out_ref[:, pl.ds(at, TILE), :] = rows.reshape(gate // TILE, TILE, gate)


def last_input(x_ref, array, gate, blocks):
    tiles = gate // TILE // blocks
    columns = []
    for a1 in range(blocks):
        parts = [
            x_ref[pl.ds(a1 * tiles, tiles), pl.ds((array * 2 + part) * blocks * TILE, blocks * TILE), :].reshape(gate, gate)
            for part in range(2)
        ]
        columns.append(jnp.concatenate(parts, axis=0))
    return jnp.concatenate(columns, axis=1)


def middle_input(x, gate, blocks):
    rows = []
    for a1 in range(blocks):
        columns = x[:, a1 * gate : (a1 + 1) * gate]
        rows.append(jnp.concatenate([columns[:gate], columns[gate:]], axis=1))
    return jnp.concatenate(rows, axis=0)


def first_input(x, gate, blocks):
    x = x.reshape(gate // TILE, blocks, TILE, 2 * gate)
    columns = []
    for c in range(blocks):
        rows = x[:, c].reshape(gate, 2 * gate)
        columns.append(jnp.concatenate([rows[:, :gate], rows[:, gate:]], axis=0))
    return jnp.concatenate(columns, axis=1)


def undo_body(gate, blocks, leave, x_ref, gates_ref, *out_refs):
    for array in range(2):
        x = left(gates_ref[2], last_input(x_ref, array, gate, blocks))
        x = right(middle_input(x, gate, blocks), gates_ref[1])
        x = left(gates_ref[0], first_input(x, gate, blocks))
        for part in range(2):
            for c in range(blocks):
                rows = x[part * gate : (part + 1) * gate, c * gate : (c + 1) * gate]
                if leave:
                    out_refs[array][pl.ds(c * 2 + part, gate, stride=2 * blocks), :] = rows
                else:
                    at = ((array * 2 + part) * blocks + c) * TILE
                    out_refs[0][:, pl.ds(at, TILE), :] = rows.reshape(gate // TILE, TILE, gate)


def pair(x, gate):
    real = x[:gate, :gate] + x[gate:, gate:]
    imag = x[gate:, :gate] - x[:gate, gate:]
    return real, imag


def gradient_body(gate, blocks, factor, x_ref, gates_ref, bit_ref, out_ref, all_ref):
    adjoint = last_input(x_ref, 1, gate, blocks)
    state = left(gates_ref[2], last_input(x_ref, 0, gate, blocks))
    permutation = order(gate, blocks)
    last = pair(contract(halves(adjoint), halves(state), ((1,), (1,))), gate)
    last = [exact(exact(permutation, u, ((1,), (0,))), permutation, ((1,), (1,))) for u in last]
    adjoint = middle_input(left(gates_ref[2], adjoint), gate, blocks)
    state = right(middle_input(state, gate, blocks), gates_ref[1])
    middle = pair(contract(halves(adjoint), halves(state), ((0,), (0,))), gate)
    adjoint = first_input(right(adjoint, gates_ref[1]), gate, blocks)
    state = left(gates_ref[0], first_input(state, gate, blocks))
    first = pair(contract(halves(adjoint), halves(state), ((1,), (1,))), gate)
    for position, grads in enumerate((first, middle, last)):
        for part in range(2):
            all_ref[pl.ds((position * 2 + part) * gate, gate), :] = factor * grads[part]
    part_out(all_ref, bit_ref[0], out_ref)


def part_out(ref, bit, out_ref):
    size = ref.shape[0] // 2
    out_ref[0] = ref[pl.ds(pl.multiple_of(bit * size, TILE), size), :]
    out_ref[1] = ref[pl.ds(pl.multiple_of((1 - bit) * size, TILE), size), :]


def add_body(kept_ref, got_ref, bit_ref, out_ref, all_ref):
    all_ref[...] = kept_ref[0] + got_ref[...]
    part_out(all_ref, bit_ref[0], out_ref)


def join_body(own_ref, got_ref, bit_ref, out_ref):
    out_ref[bit_ref[0]] = own_ref[...]
    out_ref[1 - bit_ref[0]] = got_ref[...]


def exchange(x, shards, step):
    return lax.ppermute(x, "qa", [(i, i ^ step) for i in range(shards)])


def bit_of(index, step):
    return ((index // step) % 2).astype(jnp.int32).reshape(1)


def summed(kept, shards, index):
    steps = [1 << k for k in range(shards.bit_length() - 1)]
    size = kept.shape[1]
    got = exchange(kept[1], shards, steps[0])
    shape = jax.ShapeDtypeStruct((2, size // 2, kept.shape[2]), F32)
    kept = call(
        add_body, shape, (kept, got, bit_of(index, steps[1])), 0, [VMEM, VMEM, SMEM],
        [pltpu.VMEM((size, kept.shape[2]), F32)],
    )
    total = kept[0] + exchange(kept[1], shards, steps[1])
    for step in steps[2:]:
        total = total + exchange(total, shards, step)
    for step in (steps[1], steps[0]):
        shape = jax.ShapeDtypeStruct((2, *total.shape), F32)
        joined = call(
            join_body, shape, (total, exchange(total, shards, step), bit_of(index, step)), 0, [VMEM, VMEM, SMEM]
        )
        total = joined.reshape(2 * total.shape[0], total.shape[1])
    return total


def swapped(x, shards, gate):
    tiles, rows, _ = x.shape
    groups = rows // TILE
    if shards != tiles:
        x = x.reshape(tiles, groups, TILE, gate).swapaxes(0, 1).reshape(groups, shards, gate // shards, gate).swapaxes(0, 1)
    x = lax.all_to_all(x, "qa", split_axis=0, concat_axis=0, tiled=True)
    if shards != tiles:
        x = x.swapaxes(0, 1).reshape(groups, tiles, TILE, gate).swapaxes(0, 1).reshape(tiles, rows, gate)
    return x


def on_device(state, adjoint, gates):
    rounds, _, _, _, gate = gates.shape
    local_size = state.shape[1]
    shards = lax.axis_size("qa")
    index = lax.axis_index("qa")
    blocks = local_size // (gate * gate)
    factor = 1.0 / math.sqrt(shards * local_size // gate)
    tiles = gate // TILE
    rows = blocks * gate
    flat = jax.ShapeDtypeStruct((2 * rows, gate), F32)
    tiled = jax.ShapeDtypeStruct((tiles, 4 * blocks * TILE, gate), F32)
    work = 12 * 2 * 3 * 4 * local_size * gate // 6

    matrices = call(
        functools.partial(prepare_body, rounds, gate, blocks),
        jax.ShapeDtypeStruct((rounds, 3, 2, 2 * gate, 2 * gate), BF16),
        (gates,),
        rounds * 12 * 2 * gate**3,
    )

    def entering(x):
        return x.reshape(2, rows, gate).swapaxes(0, 1).reshape(2 * rows, gate)

    def leaving(x):
        return x.reshape(rows, 2, gate).swapaxes(0, 1).reshape(2, local_size)

    x = call(functools.partial(enter_body, gate, blocks), tiled, (entering(state), entering(adjoint)), 0)
    grads = []
    for number in reversed(range(rounds)):
        x = swapped(x, shards, gate)
        matrix = matrices[number]
        parts = call(
            functools.partial(gradient_body, gate, blocks, factor),
            jax.ShapeDtypeStruct((2, 3 * gate, gate), F32),
            (x, matrix, bit_of(index, 1)),
            work,
            [VMEM, VMEM, SMEM],
            [pltpu.VMEM((6 * gate, gate), F32)],
        )
        grads.append(summed(parts, shards, index))
        x = call(
            functools.partial(undo_body, gate, blocks, number == 0),
            (flat, flat) if number == 0 else (tiled,),
            (x, matrix),
            work,
        )
        if number > 0:
            x = x[0]
    grads = jnp.stack(grads[::-1]).reshape(gates.shape)
    return leaving(x[0]), leaving(x[1]), grads


def solution(mesh):
    return jax.shard_map(
        on_device,
        mesh=mesh,
        in_specs=(P(None, ("grp", "qa")), P(None, ("grp", "qa")), P("grp", None, None, None, None)),
        out_specs=(
            P(None, ("grp", "qa")),
            P(None, ("grp", "qa")),
            P("grp", None, None, None, None),
        ),
        check_vma=False,
    )
```

```python
import functools
import math

import jax
import jax.numpy as jnp
from jax import lax
from jax.experimental import pallas as pl
from jax.experimental.pallas import tpu as pltpu
from jax.sharding import PartitionSpec as P

TILE = 8
VMEM = pl.BlockSpec(memory_space=pltpu.VMEM)
ANY = pl.BlockSpec(memory_space=pl.ANY)
SMEM = pl.BlockSpec(memory_space=pltpu.SMEM)
DEPTHS = (3, 2)
F32 = jnp.float32
BF16 = jnp.bfloat16


def call(body, out_shape, operands, flops, in_specs=None, out_spec=VMEM, scratch=(), after=(), aliases=None):
    outs = jax.tree.leaves(out_shape)
    moved = sum(math.prod(a.shape) * a.dtype.itemsize for a in (*operands, *outs))
    read = len(operands)

    def whole(*refs):
        body(*refs[:read], *refs[read + len(after) :])

    return pl.pallas_call(
        whole,
        out_shape=out_shape,
        in_specs=[*(in_specs or [VMEM] * read), *[ANY] * len(after)],
        out_specs=jax.tree.map(lambda _: out_spec, out_shape),
        scratch_shapes=scratch,
        input_output_aliases=aliases or {},
        compiler_params=pltpu.CompilerParams(vmem_limit_bytes=24 << 20),
        cost_estimate=pl.CostEstimate(flops=flops, bytes_accessed=moved, transcendentals=0),
    )(*operands, *after)


def halves(x):
    high = x.astype(BF16)
    return high, (x - high.astype(F32)).astype(BF16)


def contract(first, second, dims):
    dot = functools.partial(
        lax.dot_general, dimension_numbers=(dims, ((), ())), preferred_element_type=F32
    )
    return dot(first[0], second[0]) + (dot(first[0], second[1]) + dot(first[1], second[0]))


def left(matrix, x):
    return contract((matrix[0], matrix[1]), halves(x), ((1,), (0,)))


def right(x, matrix):
    return contract(halves(x), (matrix[0], matrix[1]), ((1,), (0,)))


def order(gate, blocks):
    rows = lax.broadcasted_iota(jnp.int32, (gate, gate), 0)
    columns = lax.broadcasted_iota(jnp.int32, (gate, gate), 1)
    inside = columns % TILE
    middle = (columns // TILE) % blocks
    tile = columns // (TILE * blocks)
    return jnp.where(rows == (tile * TILE + inside) * blocks + middle, 1.0, 0.0).astype(BF16)


def exact(first, second, dims):
    return lax.dot_general(
        first, second, (dims, ((), ())), precision=lax.Precision.HIGHEST, preferred_element_type=F32
    )


def prepare_body(rounds, gate, blocks, gates_ref, *out_refs):
    permutation = order(gate, blocks).astype(F32)
    for number in range(rounds):
        for position in range(3):
            real = gates_ref[number, position, 0]
            imag = gates_ref[number, position, 1]
            if position == 2:
                real, imag = (
                    exact(exact(permutation, u, ((0,), (0,))), permutation, ((1,), (0,))) for u in (real, imag)
                )
            if position == 1:
                quarters = ((real, -imag), (imag, real))
            else:
                real, imag = real.T, imag.T
                quarters = ((real, imag), (-imag, real))
            for i in range(2):
                for j in range(2):
                    for half, value in enumerate(halves(quarters[i][j])):
                        out_refs[number][position, half, pl.ds(i * gate, gate), pl.ds(j * gate, gate)] = value


def enter_body(gate, blocks, state_ref, adjoint_ref, out_ref, held_ref, tiles_ref, sems):
    size = 2 * blocks * TILE
    copies_in, copies_out = [], []
    for array, ref in enumerate((state_ref, adjoint_ref)):
        copies_in.append(pltpu.make_async_copy(ref, held_ref.at[array], sems.at[array]))
        at = pl.ds(array * size, size)
        copies_out.append(pltpu.make_async_copy(tiles_ref.at[:, at, :], out_ref.at[:, at, :], sems.at[2 + array]))
    for copy in copies_in:
        copy.start()
    for array in range(2):
        copies_in[array].wait()
        for part in range(2):
            for c in range(blocks):
                rows = held_ref[array, pl.ds(c * 2 + part, gate, stride=2 * blocks), :]
                at = ((array * 2 + part) * blocks + c) * TILE
                tiles_ref[:, pl.ds(at, TILE), :] = rows.reshape(gate // TILE, TILE, gate)
        copies_out[array].start()
    for copy in copies_out:
        copy.wait()


def last_input(x_ref, gate, blocks):
    tiles = gate // TILE // blocks
    size = blocks * TILE
    columns = []
    for array in range(2):
        for a1 in range(blocks):
            parts = [
                x_ref[pl.ds(a1 * tiles, tiles), pl.ds((array * 2 + part) * size, size), :].reshape(gate, gate)
                for part in range(2)
            ]
            columns.append(jnp.concatenate(parts, axis=0))
    return jnp.concatenate(columns, axis=1)


def middle_input(x, gate):
    rows = []
    for at in range(0, x.shape[1], gate):
        columns = x[:, at : at + gate]
        rows.append(jnp.concatenate([columns[:gate], columns[gate:]], axis=1))
    return jnp.concatenate(rows, axis=0)


def first_input(x, gate, blocks):
    columns = []
    for at in range(0, x.shape[0], blocks * gate):
        tiles = x[at : at + blocks * gate].reshape(gate // TILE, blocks, TILE, 2 * gate)
        for c in range(blocks):
            rows = tiles[:, c].reshape(gate, 2 * gate)
            columns.append(jnp.concatenate([rows[:, :gate], rows[:, gate:]], axis=0))
    return jnp.concatenate(columns, axis=1)


def undone(x_ref, gates_ref, gate, blocks):
    x = left(gates_ref[2], last_input(x_ref, gate, blocks))
    x = right(middle_input(x, gate), gates_ref[1])
    return left(gates_ref[0], first_input(x, gate, blocks))


def piece(x, gate, blocks, array, part, c):
    at = (array * blocks + c) * gate
    return x[part * gate : (part + 1) * gate, at : at + gate]


def undo_body(gate, blocks, x_ref, gates_ref, out_ref, tiles_ref, sems):
    x = undone(x_ref, gates_ref, gate, blocks)
    size = 2 * blocks * TILE
    copies = []
    for array in range(2):
        for part in range(2):
            for c in range(blocks):
                rows = piece(x, gate, blocks, array, part, c).reshape(gate // TILE, TILE, gate)
                tiles_ref[:, pl.ds(((array * 2 + part) * blocks + c) * TILE, TILE), :] = rows
        at = pl.ds(array * size, size)
        copies.append(pltpu.make_async_copy(tiles_ref.at[:, at, :], out_ref.at[:, at, :], sems.at[array]))
        copies[-1].start()
    for copy in copies:
        copy.wait()


def leave_body(gate, blocks, x_ref, gates_ref, state_ref, adjoint_ref, over_ref):
    x = undone(x_ref, gates_ref, gate, blocks)
    for array, ref in enumerate((state_ref, adjoint_ref)):
        for part in range(2):
            for c in range(blocks):
                ref[pl.ds(c * 2 + part, gate, stride=2 * blocks), :] = piece(x, gate, blocks, array, part, c)
    over_ref[...] = jnp.zeros_like(over_ref)


def pair(x, gate):
    real = x[:gate, :gate] + x[gate:, gate:]
    imag = x[gate:, :gate] - x[:gate, gate:]
    return real, imag


def gradient_body(gate, blocks, factor, depth, x_ref, gates_ref, bits_ref, own_ref, other_ref, all_ref):
    size = blocks * gate
    raw = last_input(x_ref, gate, blocks)
    x = left(gates_ref[2], raw)
    last = contract(halves(raw[:, size:]), halves(x[:, :size]), ((1,), (1,)))
    x = middle_input(x, gate)
    y = right(x, gates_ref[1])
    middle = contract(halves(x[size:]), halves(y[:size]), ((0,), (0,)))
    x = first_input(y, gate, blocks)
    first = contract(halves(x[:, size:]), halves(left(gates_ref[0], x[:, :size])), ((1,), (1,)))
    for position, grads in enumerate((first, middle)):
        for part, value in enumerate(pair(grads, gate)):
            all_ref[pl.ds((position * 2 + part) * gate, gate), :] = factor * value
    permutation = order(gate, blocks)
    last = halves(factor * jnp.concatenate(pair(last, gate), axis=0))
    dot = functools.partial(lax.dot_general, dimension_numbers=(((1,), (1,)), ((), ())), preferred_element_type=F32)
    last = dot(last[0], permutation) + dot(last[1], permutation)
    for part in range(2):
        for tile in range(gate // TILE // blocks):
            for c in range(blocks):
                at = part * gate + (tile * blocks + c) * TILE
                to = (4 + part) * gate + tile * TILE * blocks + c
                all_ref[pl.ds(to, TILE, stride=blocks), :] = last[at : at + TILE]
    for away, ref in enumerate((own_ref, other_ref)):
        for at, to, size in pieces(bits_ref, depth, away, all_ref.shape[0]):
            ref[pl.ds(at, size), :] = all_ref[pl.ds(to, size), :]


def pieces(bits_ref, depth, away, rows):
    size = rows >> depth
    for place in range(1 << (depth - 1)):
        at = bits_ref[0] ^ away
        for k in range(1, depth):
            at = 2 * at + (bits_ref[k] ^ (place >> (depth - 1 - k) & 1))
        yield place * size, pl.multiple_of(at * size, TILE), size


def place_body(groups, bits_ref, *refs):
    out_ref, sems = refs[-2:]
    copies = []
    for at, (rounds, depth) in enumerate(groups):
        for away in range(2):
            for start, to, size in pieces(bits_ref, depth, away, out_ref.shape[1]):
                for place, number in enumerate(rounds):
                    copies.append(
                        pltpu.make_async_copy(
                            refs[2 * at + away].at[pl.ds(start * len(rounds) + place * size, size), :],
                            out_ref.at[number, pl.ds(to, size), :],
                            sems.at[len(copies)],
                        )
                    )
    for copy in copies:
        copy.start()
    for copy in copies:
        copy.wait()


def add_body(first_ref, second_ref, out_ref):
    out_ref[...] = first_ref[...] + second_ref[...]


def add(first, second, *after):
    return call(add_body, jax.ShapeDtypeStruct(first.shape, F32), (first, second), 0, after=after)


def join_body(first_ref, second_ref, out_ref):
    size = first_ref.shape[0]
    out_ref[pl.ds(0, size), :] = first_ref[...]
    out_ref[pl.ds(size, size), :] = second_ref[...]


def join(first, second, *after):
    shape = jax.ShapeDtypeStruct((2 * first.shape[0], first.shape[1]), F32)
    return call(join_body, shape, (first, second), 0, after=after)


def exchange(x, shards, step):
    return lax.ppermute(x, "qa", [(i, i ^ step) for i in range(shards)])


def halved(total, shards, step):
    size = total.shape[0] // 2
    return total[:size] + exchange(total[size:], shards, step)


def doubled(total, shards, depth):
    for k in reversed(range(1, depth)):
        total = jnp.concatenate([total, exchange(total, shards, 1 << k)])
    return total, exchange(total, shards, 1)


def swapped(x, shards, gate):
    tiles, rows, _ = x.shape
    groups = rows // TILE
    if shards != tiles:
        x = x.reshape(tiles, groups, TILE, gate).swapaxes(0, 1).reshape(groups, shards, gate // shards, gate).swapaxes(0, 1)
    x = lax.all_to_all(x, "qa", split_axis=0, concat_axis=0, tiled=True)
    if shards != tiles:
        x = x.swapaxes(0, 1).reshape(groups, tiles, TILE, gate).swapaxes(0, 1).reshape(tiles, rows, gate)
    return x


def on_device(state, adjoint, gates):
    rounds, _, _, _, gate = gates.shape
    local_size = state.shape[1]
    shards = lax.axis_size("qa")
    index = lax.axis_index("qa")
    blocks = local_size // (gate * gate)
    factor = 1.0 / math.sqrt(shards * local_size // gate)
    tiles = gate // TILE
    rows = blocks * gate
    flat = jax.ShapeDtypeStruct((2 * rows, gate), F32)
    tiled = jax.ShapeDtypeStruct((tiles, 4 * blocks * TILE, gate), F32)
    work = 12 * 2 * 3 * 4 * local_size * gate // 6

    matrices = call(
        functools.partial(prepare_body, rounds, gate, blocks),
        [jax.ShapeDtypeStruct((3, 2, 2 * gate, 2 * gate), BF16)] * rounds,
        (gates,),
        rounds * 12 * 2 * gate**3,
    )
    bits = jnp.stack([index >> k & 1 for k in range(max(DEPTHS))]).astype(jnp.int32)

    def entering(x):
        return x.reshape(2, rows, gate).swapaxes(0, 1).reshape(2 * rows, gate)

    def leaving(x):
        return x.reshape(rows, 2, gate).swapaxes(0, 1).reshape(2, local_size)

    x = call(
        functools.partial(enter_body, gate, blocks),
        tiled,
        [pltpu.with_memory_space_constraint(entering(array), pltpu.HBM) for array in (state, adjoint)],
        0,
        [ANY, ANY],
        ANY,
        [
            pltpu.VMEM((2, 2 * rows, gate), F32),
            pltpu.VMEM(tiled.shape, F32),
            pltpu.SemaphoreType.DMA((4,)),
        ],
    )
    steps = [1 << k for k in range(shards.bit_length() - 1)]
    early_depth, late_depth = DEPTHS
    totals, left_over = [], []
    for number in reversed(range(rounds)):
        x = swapped(x, shards, gate)
        if number < rounds - 1:
            for at in range(len(totals)):
                if number == 0 or at < len(totals) - 1:
                    for step in left_over[at]:
                        totals[at] = halved(totals[at], shards, step)
                    left_over[at] = []
        own, other = call(
            functools.partial(gradient_body, gate, blocks, factor, early_depth if number > 0 else late_depth),
            [jax.ShapeDtypeStruct((3 * gate, gate), F32)] * 2,
            (x, matrices[number], bits),
            work,
            [VMEM, VMEM, SMEM],
            scratch=[pltpu.VMEM((6 * gate, gate), F32)],
            after=totals if number == 0 else (),
        )
        total = own + exchange(other, shards, steps[0])
        if number > 0:
            x = call(
                functools.partial(undo_body, gate, blocks),
                tiled,
                (x, matrices[number]),
                work,
                out_spec=ANY,
                scratch=[pltpu.VMEM(tiled.shape, F32), pltpu.SemaphoreType.DMA((2,))],
                after=totals,
            )
            totals.append(halved(total, shards, steps[1]))
            left_over.append(steps[2:early_depth])
    token = jax.ShapeDtypeStruct((TILE, gate), F32)
    state, adjoint, over = call(
        functools.partial(leave_body, gate, blocks), [flat, flat, token], (x, matrices[0]), work, after=totals
    )
    early, late = jnp.concatenate(totals), total
    for step in steps[1:late_depth]:
        late = halved(late, shards, step)
    for step in steps[early_depth:]:
        early = early + exchange(early, shards, step)
    for step in steps[late_depth:-1]:
        late = late + exchange(late, shards, step)
    late = add(late, exchange(late, shards, steps[-1]), over)
    groups = ((tuple(reversed(range(1, rounds))), early_depth), ((0,), late_depth))
    grads = call(
        functools.partial(place_body, groups),
        jax.ShapeDtypeStruct((rounds, 6 * gate, gate), F32),
        (bits, *doubled(early, shards, early_depth), *doubled(late, shards, late_depth)),
        0,
        [SMEM] + [ANY] * 4,
        ANY,
        [pltpu.SemaphoreType.DMA((rounds << early_depth,))],
    )
    return leaving(state), leaving(adjoint), grads.reshape(gates.shape)


def solution(mesh):
    return jax.shard_map(
        on_device,
        mesh=mesh,
        in_specs=(P(None, ("grp", "qa")), P(None, ("grp", "qa")), P("grp", None, None, None, None)),
        out_specs=(
            P(None, ("grp", "qa")),
            P(None, ("grp", "qa")),
            P("grp", None, None, None, None),
        ),
        check_vma=False,
    )
```

```python
import functools
import math

import jax
import jax.numpy as jnp
from jax import lax
from jax.experimental import pallas as pl
from jax.experimental.pallas import tpu as pltpu
from jax.sharding import PartitionSpec as P

TILE = 8
VMEM = pl.BlockSpec(memory_space=pltpu.VMEM)
ANY = pl.BlockSpec(memory_space=pl.ANY)
SMEM = pl.BlockSpec(memory_space=pltpu.SMEM)
DEPTHS = (3, 2)
F32 = jnp.float32
BF16 = jnp.bfloat16


def call(body, out_shape, operands, flops, in_specs=None, out_spec=VMEM, scratch=(), after=(), aliases=None):
    outs = jax.tree.leaves(out_shape)
    moved = sum(math.prod(a.shape) * a.dtype.itemsize for a in (*operands, *outs))
    read = len(operands)

    def whole(*refs):
        body(*refs[:read], *refs[read + len(after) :])

    return pl.pallas_call(
        whole,
        out_shape=out_shape,
        in_specs=[*(in_specs or [VMEM] * read), *[ANY] * len(after)],
        out_specs=jax.tree.map(lambda _: out_spec, out_shape),
        scratch_shapes=scratch,
        input_output_aliases=aliases or {},
        compiler_params=pltpu.CompilerParams(vmem_limit_bytes=24 << 20),
        cost_estimate=pl.CostEstimate(flops=flops, bytes_accessed=moved, transcendentals=0),
    )(*operands, *after)


def halves(x):
    high = x.astype(BF16)
    return high, (x - high.astype(F32)).astype(BF16)


def contract(first, second, dims):
    dot = functools.partial(
        lax.dot_general, dimension_numbers=(dims, ((), ())), preferred_element_type=F32
    )
    return dot(first[0], second[0]) + (dot(first[0], second[1]) + dot(first[1], second[0]))


def left(matrix, x):
    return contract((matrix[0], matrix[1]), halves(x), ((1,), (0,)))


def right(x, matrix):
    return contract(halves(x), (matrix[0], matrix[1]), ((1,), (0,)))


def order(gate, blocks):
    rows = lax.broadcasted_iota(jnp.int32, (gate, gate), 0)
    columns = lax.broadcasted_iota(jnp.int32, (gate, gate), 1)
    inside = columns % TILE
    middle = (columns // TILE) % blocks
    tile = columns // (TILE * blocks)
    return jnp.where(rows == (tile * TILE + inside) * blocks + middle, 1.0, 0.0).astype(BF16)


def exact(first, second, dims):
    return lax.dot_general(
        first, second, (dims, ((), ())), precision=lax.Precision.HIGHEST, preferred_element_type=F32
    )


def prepare_body(rounds, gate, blocks, gates_ref, *out_refs):
    permutation = order(gate, blocks).astype(F32)
    for number in range(rounds):
        for position in range(3):
            real = gates_ref[number, position, 0]
            imag = gates_ref[number, position, 1]
            if position == 2:
                real, imag = (
                    exact(exact(permutation, u, ((0,), (0,))), permutation, ((1,), (0,))) for u in (real, imag)
                )
            if position == 1:
                quarters = ((real, -imag), (imag, real))
            else:
                real, imag = real.T, imag.T
                quarters = ((real, imag), (-imag, real))
            for i in range(2):
                for j in range(2):
                    for half, value in enumerate(halves(quarters[i][j])):
                        out_refs[number][position, half, pl.ds(i * gate, gate), pl.ds(j * gate, gate)] = value


def enter_body(gate, blocks, state_ref, adjoint_ref, out_ref, held_ref, tiles_ref, sems):
    size = 2 * blocks * TILE
    copies_in, copies_out = [], []
    for array, ref in enumerate((state_ref, adjoint_ref)):
        copies_in.append(pltpu.make_async_copy(ref, held_ref.at[array], sems.at[array]))
        at = pl.ds(array * size, size)
        copies_out.append(pltpu.make_async_copy(tiles_ref.at[:, at, :], out_ref.at[:, at, :], sems.at[2 + array]))
    for copy in copies_in:
        copy.start()
    for array in range(2):
        copies_in[array].wait()
        for part in range(2):
            for c in range(blocks):
                rows = held_ref[array, pl.ds(c * 2 + part, gate, stride=2 * blocks), :]
                at = ((array * 2 + part) * blocks + c) * TILE
                tiles_ref[:, pl.ds(at, TILE), :] = rows.reshape(gate // TILE, TILE, gate)
        copies_out[array].start()
    for copy in copies_out:
        copy.wait()


def last_input(x_ref, gate, blocks):
    tiles = gate // TILE // blocks
    size = blocks * TILE
    columns = []
    for array in range(2):
        for a1 in range(blocks):
            parts = [
                x_ref[pl.ds(a1 * tiles, tiles), pl.ds((array * 2 + part) * size, size), :].reshape(gate, gate)
                for part in range(2)
            ]
            columns.append(jnp.concatenate(parts, axis=0))
    return jnp.concatenate(columns, axis=1)


def middle_input(x, gate):
    rows = []
    for at in range(0, x.shape[1], gate):
        columns = x[:, at : at + gate]
        rows.append(jnp.concatenate([columns[:gate], columns[gate:]], axis=1))
    return jnp.concatenate(rows, axis=0)


def first_input(x, gate, blocks):
    columns = []
    for at in range(0, x.shape[0], blocks * gate):
        tiles = x[at : at + blocks * gate].reshape(gate // TILE, blocks, TILE, 2 * gate)
        for c in range(blocks):
            rows = tiles[:, c].reshape(gate, 2 * gate)
            columns.append(jnp.concatenate([rows[:, :gate], rows[:, gate:]], axis=0))
    return jnp.concatenate(columns, axis=1)


def undone(x_ref, gates_ref, gate, blocks):
    x = left(gates_ref[2], last_input(x_ref, gate, blocks))
    x = right(middle_input(x, gate), gates_ref[1])
    return left(gates_ref[0], first_input(x, gate, blocks))


def piece(x, gate, blocks, array, part, c):
    at = (array * blocks + c) * gate
    return x[part * gate : (part + 1) * gate, at : at + gate]


def undo_body(gate, blocks, x_ref, gates_ref, out_ref, tiles_ref, sems):
    x = undone(x_ref, gates_ref, gate, blocks)
    size = 2 * blocks * TILE
    copies = []
    for array in range(2):
        for part in range(2):
            for c in range(blocks):
                rows = piece(x, gate, blocks, array, part, c).reshape(gate // TILE, TILE, gate)
                tiles_ref[:, pl.ds(((array * 2 + part) * blocks + c) * TILE, TILE), :] = rows
        at = pl.ds(array * size, size)
        copies.append(pltpu.make_async_copy(tiles_ref.at[:, at, :], out_ref.at[:, at, :], sems.at[array]))
        copies[-1].start()
    for copy in copies:
        copy.wait()


def leave_body(gate, blocks, x_ref, gates_ref, state_ref, adjoint_ref, over_ref):
    x = undone(x_ref, gates_ref, gate, blocks)
    for array, ref in enumerate((state_ref, adjoint_ref)):
        for part in range(2):
            for c in range(blocks):
                ref[pl.ds(c * 2 + part, gate, stride=2 * blocks), :] = piece(x, gate, blocks, array, part, c)
    over_ref[...] = jnp.zeros_like(over_ref)


def pair(x, gate):
    real = x[:gate, :gate] + x[gate:, gate:]
    imag = x[gate:, :gate] - x[:gate, gate:]
    return real, imag


def gradient_body(gate, blocks, factor, depth, x_ref, gates_ref, bits_ref, own_ref, other_ref, all_ref):
    size = blocks * gate
    raw = last_input(x_ref, gate, blocks)
    x = left(gates_ref[2], raw)
    last = contract(halves(raw[:, size:]), halves(x[:, :size]), ((1,), (1,)))
    x = middle_input(x, gate)
    y = right(x, gates_ref[1])
    middle = contract(halves(x[size:]), halves(y[:size]), ((0,), (0,)))
    x = first_input(y, gate, blocks)
    first = contract(halves(x[:, size:]), halves(left(gates_ref[0], x[:, :size])), ((1,), (1,)))
    for position, grads in enumerate((first, middle)):
        for part, value in enumerate(pair(grads, gate)):
            all_ref[pl.ds((position * 2 + part) * gate, gate), :] = factor * value
    permutation = order(gate, blocks)
    last = halves(factor * jnp.concatenate(pair(last, gate), axis=0))
    dot = functools.partial(lax.dot_general, dimension_numbers=(((1,), (1,)), ((), ())), preferred_element_type=F32)
    last = dot(last[0], permutation) + dot(last[1], permutation)
    for part in range(2):
        for tile in range(gate // TILE // blocks):
            for c in range(blocks):
                at = part * gate + (tile * blocks + c) * TILE
                to = (4 + part) * gate + tile * TILE * blocks + c
                all_ref[pl.ds(to, TILE, stride=blocks), :] = last[at : at + TILE]
    for away, ref in enumerate((own_ref, other_ref)):
        for at, to, size in pieces(bits_ref, depth, away, all_ref.shape[0]):
            ref[pl.ds(at, size), :] = all_ref[pl.ds(to, size), :]


def pieces(bits_ref, depth, away, rows):
    size = rows >> depth
    for place in range(1 << (depth - 1)):
        at = bits_ref[0] ^ away
        for k in range(1, depth):
            at = 2 * at + (bits_ref[k] ^ (place >> (depth - 1 - k) & 1))
        yield place * size, pl.multiple_of(at * size, TILE), size


def place_body(groups, bits_ref, *refs):
    out_ref, sems = refs[-2:]
    copies = []
    for at, (rounds, depth) in enumerate(groups):
        for away in range(2):
            for start, to, size in pieces(bits_ref, depth, away, out_ref.shape[1]):
                for place, number in enumerate(rounds):
                    copies.append(
                        pltpu.make_async_copy(
                            refs[2 * at + away].at[pl.ds(start * len(rounds) + place * size, size), :],
                            out_ref.at[number, pl.ds(to, size), :],
                            sems.at[len(copies)],
                        )
                    )
    for copy in copies:
        copy.start()
    for copy in copies:
        copy.wait()


def add_body(first_ref, second_ref, out_ref):
    out_ref[...] = first_ref[...] + second_ref[...]


def add(first, second, *after):
    return call(add_body, jax.ShapeDtypeStruct(first.shape, F32), (first, second), 0, after=after)


def join_body(first_ref, second_ref, out_ref):
    size = first_ref.shape[0]
    out_ref[pl.ds(0, size), :] = first_ref[...]
    out_ref[pl.ds(size, size), :] = second_ref[...]


def join(first, second, *after):
    shape = jax.ShapeDtypeStruct((2 * first.shape[0], first.shape[1]), F32)
    return call(join_body, shape, (first, second), 0, after=after)


def exchange(x, shards, step):
    return lax.ppermute(x, "qa", [(i, i ^ step) for i in range(shards)])


def halved(total, shards, step):
    size = total.shape[0] // 2
    return total[:size] + exchange(total[size:], shards, step)


def doubled(total, shards, depth):
    for k in reversed(range(1, depth)):
        total = jnp.concatenate([total, exchange(total, shards, 1 << k)])
    return total, exchange(total, shards, 1)


def swapped(x, shards, gate):
    tiles, rows, _ = x.shape
    groups = rows // TILE
    if shards != tiles:
        x = x.reshape(tiles, groups, TILE, gate).swapaxes(0, 1).reshape(groups, shards, gate // shards, gate).swapaxes(0, 1)
    x = lax.all_to_all(x, "qa", split_axis=0, concat_axis=0, tiled=True)
    if shards != tiles:
        x = x.swapaxes(0, 1).reshape(groups, tiles, TILE, gate).swapaxes(0, 1).reshape(tiles, rows, gate)
    return x


def on_device(state, adjoint, gates):
    rounds, _, _, _, gate = gates.shape
    local_size = state.shape[1]
    shards = lax.axis_size("qa")
    index = lax.axis_index("qa")
    blocks = local_size // (gate * gate)
    factor = 1.0 / math.sqrt(shards * local_size // gate)
    tiles = gate // TILE
    rows = blocks * gate
    flat = jax.ShapeDtypeStruct((2 * rows, gate), F32)
    tiled = jax.ShapeDtypeStruct((tiles, 4 * blocks * TILE, gate), F32)
    work = 48 * local_size * gate

    matrices = call(
        functools.partial(prepare_body, rounds, gate, blocks),
        [jax.ShapeDtypeStruct((3, 2, 2 * gate, 2 * gate), BF16)] * rounds,
        (gates,),
        rounds * 12 * 2 * gate**3,
    )
    steps = [1 << k for k in range(shards.bit_length() - 1)]
    early_depth, late_depth = DEPTHS
    stepwise = shards == 1 << len(steps) and len(steps) >= max(DEPTHS)
    bits = jnp.stack([index >> k & 1 if stepwise else index * 0 for k in range(max(DEPTHS))]).astype(jnp.int32)

    def entering(x):
        return x.reshape(2, rows, gate).swapaxes(0, 1).reshape(2 * rows, gate)

    def leaving(x):
        return x.reshape(rows, 2, gate).swapaxes(0, 1).reshape(2, local_size)

    x = call(
        functools.partial(enter_body, gate, blocks),
        tiled,
        [pltpu.with_memory_space_constraint(entering(array), pltpu.HBM) for array in (state, adjoint)],
        0,
        [ANY, ANY],
        ANY,
        [
            pltpu.VMEM((2, 2 * rows, gate), F32),
            pltpu.VMEM(tiled.shape, F32),
            pltpu.SemaphoreType.DMA((4,)),
        ],
    )
    totals, left_over, plain = [], [], []
    for number in reversed(range(rounds)):
        x = swapped(x, shards, gate)
        if number < rounds - 1:
            for at in range(len(totals)):
                if number == 0 or at < len(totals) - 1:
                    for step in left_over[at]:
                        totals[at] = halved(totals[at], shards, step)
                    left_over[at] = []
        own, other = call(
            functools.partial(gradient_body, gate, blocks, factor, early_depth if number > 0 else late_depth),
            [jax.ShapeDtypeStruct((3 * gate, gate), F32)] * 2,
            (x, matrices[number], bits),
            work,
            [VMEM, VMEM, SMEM],
            scratch=[pltpu.VMEM((6 * gate, gate), F32)],
            after=totals if number == 0 else (),
        )
        if stepwise:
            total = own + exchange(other, shards, steps[0])
        else:
            plain.append(lax.psum(jnp.concatenate([own, other]), "qa"))
        if number > 0:
            x = call(
                functools.partial(undo_body, gate, blocks),
                tiled,
                (x, matrices[number]),
                work,
                out_spec=ANY,
                scratch=[pltpu.VMEM(tiled.shape, F32), pltpu.SemaphoreType.DMA((2,))],
                after=totals,
            )
            if stepwise:
                totals.append(halved(total, shards, steps[1]))
                left_over.append(steps[2:early_depth])
    token = jax.ShapeDtypeStruct((TILE, gate), F32)
    state, adjoint, over = call(
        functools.partial(leave_body, gate, blocks), [flat, flat, token], (x, matrices[0]), work, after=totals
    )
    if not stepwise:
        return leaving(state), leaving(adjoint), jnp.stack(plain[::-1]).reshape(gates.shape)
    groups = (tuple(reversed(range(2, rounds))), (1,))
    early = []
    for group in groups:
        part = jnp.concatenate([totals[rounds - 1 - number] for number in group])
        for step in steps[early_depth:]:
            part = part + exchange(part, shards, step)
        early.append(doubled(part, shards, early_depth))
    late = total
    for step in steps[1:late_depth]:
        late = halved(late, shards, step)
    for step in steps[late_depth:-1]:
        late = late + exchange(late, shards, step)
    late = add(late, exchange(late, shards, steps[-1]), over)
    finished = [*early, doubled(late, shards, late_depth)]
    groups = (*((group, early_depth) for group in groups), ((0,), late_depth))
    grads = call(
        functools.partial(place_body, groups),
        jax.ShapeDtypeStruct((rounds, 6 * gate, gate), F32),
        (bits, *(half for pair_of in finished for half in pair_of)),
        0,
        [SMEM] + [ANY] * (2 * len(groups)),
        ANY,
        [pltpu.SemaphoreType.DMA((rounds << early_depth,))],
    )
    return leaving(state), leaving(adjoint), grads.reshape(gates.shape)


def solution(mesh):
    return jax.shard_map(
        on_device,
        mesh=mesh,
        in_specs=(P(None, ("grp", "qa")), P(None, ("grp", "qa")), P("grp", None, None, None, None)),
        out_specs=(
            P(None, ("grp", "qa")),
            P(None, ("grp", "qa")),
            P("grp", None, None, None, None),
        ),
        check_vma=False,
    )
```

```python
import functools
import math

import jax
import jax.numpy as jnp
from jax import lax
from jax.experimental import pallas as pl
from jax.experimental.pallas import tpu as pltpu
from jax.sharding import PartitionSpec as P

TILE = 8
VMEM = pl.BlockSpec(memory_space=pltpu.VMEM)
ANY = pl.BlockSpec(memory_space=pl.ANY)
SMEM = pl.BlockSpec(memory_space=pltpu.SMEM)
DEPTHS = (3, 2)
F32 = jnp.float32
BF16 = jnp.bfloat16


def call(body, out_shape, operands, flops, in_specs=None, out_spec=VMEM, scratch=(), after=(), aliases=None):
    outs = jax.tree.leaves(out_shape)
    moved = sum(math.prod(a.shape) * a.dtype.itemsize for a in (*operands, *outs))
    read = len(operands)

    def whole(*refs):
        body(*refs[:read], *refs[read + len(after) :])

    return pl.pallas_call(
        whole,
        out_shape=out_shape,
        in_specs=[*(in_specs or [VMEM] * read), *[ANY] * len(after)],
        out_specs=jax.tree.map(lambda _: out_spec, out_shape),
        scratch_shapes=scratch,
        input_output_aliases=aliases or {},
        compiler_params=pltpu.CompilerParams(vmem_limit_bytes=24 << 20),
        cost_estimate=pl.CostEstimate(flops=flops, bytes_accessed=moved, transcendentals=0),
    )(*operands, *after)


def halves(x):
    high = x.astype(BF16)
    return high, (x - high.astype(F32)).astype(BF16)


def contract(first, second, dims):
    dot = functools.partial(
        lax.dot_general, dimension_numbers=(dims, ((), ())), preferred_element_type=F32
    )
    return dot(first[0], second[0]) + (dot(first[0], second[1]) + dot(first[1], second[0]))


def left(matrix, x):
    return contract((matrix[0], matrix[1]), halves(x), ((1,), (0,)))


def right(x, matrix):
    return contract(halves(x), (matrix[0], matrix[1]), ((1,), (0,)))


def order(gate, blocks):
    rows = lax.broadcasted_iota(jnp.int32, (gate, gate), 0)
    columns = lax.broadcasted_iota(jnp.int32, (gate, gate), 1)
    inside = columns % TILE
    middle = (columns // TILE) % blocks
    tile = columns // (TILE * blocks)
    return jnp.where(rows == (tile * TILE + inside) * blocks + middle, 1.0, 0.0).astype(BF16)


def exact(first, second, dims):
    return lax.dot_general(
        first, second, (dims, ((), ())), precision=lax.Precision.HIGHEST, preferred_element_type=F32
    )


def prepare_body(rounds, gate, blocks, gates_ref, *out_refs):
    permutation = order(gate, blocks).astype(F32)
    for number in range(rounds):
        for position in range(3):
            real = gates_ref[number, position, 0]
            imag = gates_ref[number, position, 1]
            if position == 2:
                real, imag = (
                    exact(exact(permutation, u, ((0,), (0,))), permutation, ((1,), (0,))) for u in (real, imag)
                )
            if position == 1:
                quarters = ((real, -imag), (imag, real))
            else:
                real, imag = real.T, imag.T
                quarters = ((real, imag), (-imag, real))
            for i in range(2):
                for j in range(2):
                    for half, value in enumerate(halves(quarters[i][j])):
                        out_refs[number][position, half, pl.ds(i * gate, gate), pl.ds(j * gate, gate)] = value


def enter_body(gate, blocks, state_ref, adjoint_ref, out_ref, held_ref, tiles_ref, sems):
    size = 2 * blocks * TILE
    copies_in, copies_out = [], []
    for array, ref in enumerate((state_ref, adjoint_ref)):
        copies_in.append(pltpu.make_async_copy(ref, held_ref.at[array], sems.at[array]))
        at = pl.ds(array * size, size)
        copies_out.append(pltpu.make_async_copy(tiles_ref.at[:, at, :], out_ref.at[:, at, :], sems.at[2 + array]))
    for copy in copies_in:
        copy.start()
    for array in range(2):
        copies_in[array].wait()
        for part in range(2):
            for c in range(blocks):
                rows = held_ref[array, pl.ds(c * 2 + part, gate, stride=2 * blocks), :]
                at = ((array * 2 + part) * blocks + c) * TILE
                tiles_ref[:, pl.ds(at, TILE), :] = rows.reshape(gate // TILE, TILE, gate)
        copies_out[array].start()
    for copy in copies_out:
        copy.wait()


def last_input(x_ref, gate, blocks):
    tiles = gate // TILE // blocks
    size = blocks * TILE
    columns = []
    for array in range(2):
        for a1 in range(blocks):
            parts = [
                x_ref[pl.ds(a1 * tiles, tiles), pl.ds((array * 2 + part) * size, size), :].reshape(gate, gate)
                for part in range(2)
            ]
            columns.append(jnp.concatenate(parts, axis=0))
    return jnp.concatenate(columns, axis=1)


def middle_input(x, gate):
    rows = []
    for at in range(0, x.shape[1], gate):
        columns = x[:, at : at + gate]
        rows.append(jnp.concatenate([columns[:gate], columns[gate:]], axis=1))
    return jnp.concatenate(rows, axis=0)


def first_input(x, gate, blocks):
    columns = []
    for at in range(0, x.shape[0], blocks * gate):
        tiles = x[at : at + blocks * gate].reshape(gate // TILE, blocks, TILE, 2 * gate)
        for c in range(blocks):
            rows = tiles[:, c].reshape(gate, 2 * gate)
            columns.append(jnp.concatenate([rows[:, :gate], rows[:, gate:]], axis=0))
    return jnp.concatenate(columns, axis=1)


def undone(x_ref, gates_ref, gate, blocks):
    x = left(gates_ref[2], last_input(x_ref, gate, blocks))
    x = right(middle_input(x, gate), gates_ref[1])
    return left(gates_ref[0], first_input(x, gate, blocks))


def piece(x, gate, blocks, array, part, c):
    at = (array * blocks + c) * gate
    return x[part * gate : (part + 1) * gate, at : at + gate]


def undo_body(gate, blocks, x_ref, gates_ref, out_ref, tiles_ref, sems):
    x = undone(x_ref, gates_ref, gate, blocks)
    size = 2 * blocks * TILE
    copies = []
    for array in range(2):
        for part in range(2):
            for c in range(blocks):
                rows = piece(x, gate, blocks, array, part, c).reshape(gate // TILE, TILE, gate)
                tiles_ref[:, pl.ds(((array * 2 + part) * blocks + c) * TILE, TILE), :] = rows
        at = pl.ds(array * size, size)
        copies.append(pltpu.make_async_copy(tiles_ref.at[:, at, :], out_ref.at[:, at, :], sems.at[array]))
        copies[-1].start()
    for copy in copies:
        copy.wait()


def leave_body(gate, blocks, x_ref, gates_ref, state_ref, adjoint_ref, over_ref):
    x = undone(x_ref, gates_ref, gate, blocks)
    for array, ref in enumerate((state_ref, adjoint_ref)):
        for part in range(2):
            for c in range(blocks):
                ref[pl.ds(c * 2 + part, gate, stride=2 * blocks), :] = piece(x, gate, blocks, array, part, c)
    over_ref[...] = jnp.zeros_like(over_ref)


def pair(x, gate):
    real = x[:gate, :gate] + x[gate:, gate:]
    imag = x[gate:, :gate] - x[:gate, gate:]
    return real, imag


def gradient_body(gate, blocks, factor, depth, x_ref, gates_ref, bits_ref, own_ref, other_ref, all_ref):
    size = blocks * gate
    raw = last_input(x_ref, gate, blocks)
    x = left(gates_ref[2], raw)
    last = contract(halves(raw[:, size:]), halves(x[:, :size]), ((1,), (1,)))
    x = middle_input(x, gate)
    y = right(x, gates_ref[1])
    middle = contract(halves(x[size:]), halves(y[:size]), ((0,), (0,)))
    x = first_input(y, gate, blocks)
    first = contract(halves(x[:, size:]), halves(left(gates_ref[0], x[:, :size])), ((1,), (1,)))
    for position, grads in enumerate((first, middle)):
        for part, value in enumerate(pair(grads, gate)):
            all_ref[pl.ds((position * 2 + part) * gate, gate), :] = factor * value
    permutation = order(gate, blocks)
    last = halves(factor * jnp.concatenate(pair(last, gate), axis=0))
    dot = functools.partial(lax.dot_general, dimension_numbers=(((1,), (1,)), ((), ())), preferred_element_type=F32)
    last = dot(last[0], permutation) + dot(last[1], permutation)
    for part in range(2):
        for tile in range(gate // TILE // blocks):
            for c in range(blocks):
                at = part * gate + (tile * blocks + c) * TILE
                to = (4 + part) * gate + tile * TILE * blocks + c
                all_ref[pl.ds(to, TILE, stride=blocks), :] = last[at : at + TILE]
    for away, ref in enumerate((own_ref, other_ref)):
        for at, to, size in pieces(bits_ref, depth, away, all_ref.shape[0]):
            ref[pl.ds(at, size), :] = all_ref[pl.ds(to, size), :]


def pieces(bits_ref, depth, away, rows):
    size = rows >> depth
    for place in range(1 << (depth - 1)):
        at = bits_ref[0] ^ away
        for k in range(1, depth):
            at = 2 * at + (bits_ref[k] ^ (place >> (depth - 1 - k) & 1))
        yield place * size, pl.multiple_of(at * size, TILE), size


def place_body(groups, bits_ref, *refs):
    out_ref, sems = refs[-2:]
    copies = []
    for at, (rounds, depth) in enumerate(groups):
        for away in range(2):
            for start, to, size in pieces(bits_ref, depth, away, out_ref.shape[1]):
                for place, number in enumerate(rounds):
                    copies.append(
                        pltpu.make_async_copy(
                            refs[2 * at + away].at[pl.ds(start * len(rounds) + place * size, size), :],
                            out_ref.at[number, pl.ds(to, size), :],
                            sems.at[len(copies)],
                        )
                    )
    for copy in copies:
        copy.start()
    for copy in copies:
        copy.wait()


def add_body(first_ref, second_ref, out_ref):
    out_ref[...] = first_ref[...] + second_ref[...]


def add(first, second, *after):
    return call(add_body, jax.ShapeDtypeStruct(first.shape, F32), (first, second), 0, after=after)


def join_body(first_ref, second_ref, out_ref):
    size = first_ref.shape[0]
    out_ref[pl.ds(0, size), :] = first_ref[...]
    out_ref[pl.ds(size, size), :] = second_ref[...]


def join(first, second, *after):
    shape = jax.ShapeDtypeStruct((2 * first.shape[0], first.shape[1]), F32)
    return call(join_body, shape, (first, second), 0, after=after)


def exchange(x, shards, step):
    return lax.ppermute(x, "qa", [(i, i ^ step) for i in range(shards)])


def halved(total, shards, step):
    size = total.shape[0] // 2
    return total[:size] + exchange(total[size:], shards, step)


def doubled(total, shards, depth):
    for k in reversed(range(1, depth)):
        total = jnp.concatenate([total, exchange(total, shards, 1 << k)])
    return total, exchange(total, shards, 1)


def swapped(x, shards, gate):
    tiles, rows, _ = x.shape
    groups = rows // TILE
    if shards != tiles:
        x = x.reshape(tiles, groups, TILE, gate).swapaxes(0, 1).reshape(groups, shards, gate // shards, gate).swapaxes(0, 1)
    x = lax.all_to_all(x, "qa", split_axis=0, concat_axis=0, tiled=True)
    if shards != tiles:
        x = x.swapaxes(0, 1).reshape(groups, tiles, TILE, gate).swapaxes(0, 1).reshape(tiles, rows, gate)
    return x


def on_device(state, adjoint, gates):
    rounds, _, _, _, gate = gates.shape
    local_size = state.shape[1]
    shards = lax.axis_size("qa")
    index = lax.axis_index("qa")
    blocks = local_size // (gate * gate)
    factor = 1.0 / math.sqrt(shards * local_size // gate)
    tiles = gate // TILE
    rows = blocks * gate
    flat = jax.ShapeDtypeStruct((2 * rows, gate), F32)
    tiled = jax.ShapeDtypeStruct((tiles, 4 * blocks * TILE, gate), F32)
    work = 48 * local_size * gate

    matrices = call(
        functools.partial(prepare_body, rounds, gate, blocks),
        [jax.ShapeDtypeStruct((3, 2, 2 * gate, 2 * gate), BF16)] * rounds,
        (gates,),
        rounds * 12 * 2 * gate**3,
    )
    steps = [1 << k for k in range(shards.bit_length() - 1)]
    early_depth, late_depth = DEPTHS
    stepwise = shards == 1 << len(steps) and len(steps) >= max(DEPTHS)
    bits = jnp.stack([index >> k & 1 if stepwise else index * 0 for k in range(max(DEPTHS))]).astype(jnp.int32)

    def entering(x):
        return x.reshape(2, rows, gate).swapaxes(0, 1).reshape(2 * rows, gate)

    def leaving(x):
        return x.reshape(rows, 2, gate).swapaxes(0, 1).reshape(2, local_size)

    x = call(
        functools.partial(enter_body, gate, blocks),
        tiled,
        [pltpu.with_memory_space_constraint(entering(array), pltpu.HBM) for array in (state, adjoint)],
        0,
        [ANY, ANY],
        ANY,
        [
            pltpu.VMEM((2, 2 * rows, gate), F32),
            pltpu.VMEM(tiled.shape, F32),
            pltpu.SemaphoreType.DMA((4,)),
        ],
    )
    totals, left_over, plain = [], [], []
    for number in reversed(range(rounds)):
        x = swapped(x, shards, gate)
        if number < rounds - 1:
            for at in range(len(totals)):
                if number == 0 or at < len(totals) - 1:
                    for step in left_over[at]:
                        totals[at] = halved(totals[at], shards, step)
                    left_over[at] = []
        own, other = call(
            functools.partial(gradient_body, gate, blocks, factor, early_depth if number > 0 else late_depth),
            [jax.ShapeDtypeStruct((3 * gate, gate), F32)] * 2,
            (x, matrices[number], bits),
            work,
            [VMEM, VMEM, SMEM],
            scratch=[pltpu.VMEM((6 * gate, gate), F32)],
            after=totals if number == 0 else (),
        )
        if stepwise:
            total = own + exchange(other, shards, steps[0])
        else:
            plain.append(lax.psum(jnp.concatenate([own, other]), "qa"))
        if number > 0:
            x = call(
                functools.partial(undo_body, gate, blocks),
                tiled,
                (x, matrices[number]),
                work,
                out_spec=ANY,
                scratch=[pltpu.VMEM(tiled.shape, F32), pltpu.SemaphoreType.DMA((2,))],
                after=totals,
            )
            if stepwise:
                totals.append(halved(total, shards, steps[1]))
                left_over.append(steps[2:early_depth])
    token = jax.ShapeDtypeStruct((TILE, gate), F32)
    state, adjoint, over = call(
        functools.partial(leave_body, gate, blocks), [flat, flat, token], (x, matrices[0]), work, after=totals
    )
    if not stepwise:
        return leaving(state), leaving(adjoint), jnp.stack(plain[::-1]).reshape(gates.shape)
    groups = (tuple(reversed(range(2, rounds))), (1,))
    early = []
    for group in groups:
        part = jnp.concatenate([totals[rounds - 1 - number] for number in group])
        for step in steps[early_depth:]:
            part = part + exchange(part, shards, step)
        early.append(doubled(part, shards, early_depth))
    late = total
    for step in steps[1:late_depth]:
        late = halved(late, shards, step)
    for step in steps[late_depth + 1 :]:
        late = late + exchange(late, shards, step)
    late = add(late, exchange(late, shards, steps[late_depth]), over)
    finished = [*early, doubled(late, shards, late_depth)]
    groups = (*((group, early_depth) for group in groups), ((0,), late_depth))
    grads = call(
        functools.partial(place_body, groups),
        jax.ShapeDtypeStruct((rounds, 6 * gate, gate), F32),
        (bits, *(half for pair_of in finished for half in pair_of)),
        0,
        [SMEM] + [ANY] * (2 * len(groups)),
        ANY,
        [pltpu.SemaphoreType.DMA((rounds << early_depth,))],
    )
    return leaving(state), leaving(adjoint), grads.reshape(gates.shape)


def solution(mesh):
    return jax.shard_map(
        on_device,
        mesh=mesh,
        in_specs=(P(None, ("grp", "qa")), P(None, ("grp", "qa")), P("grp", None, None, None, None)),
        out_specs=(
            P(None, ("grp", "qa")),
            P(None, ("grp", "qa")),
            P("grp", None, None, None, None),
        ),
        check_vma=False,
    )
```

```python
import functools
import math

import jax
import jax.numpy as jnp
from jax import lax
from jax.experimental import pallas as pl
from jax.experimental.pallas import tpu as pltpu
from jax.sharding import PartitionSpec as P

TILE = 8
VMEM = pl.BlockSpec(memory_space=pltpu.VMEM)
ANY = pl.BlockSpec(memory_space=pl.ANY)
SMEM = pl.BlockSpec(memory_space=pltpu.SMEM)
DEPTHS = (3, 2)
F32 = jnp.float32
BF16 = jnp.bfloat16


def call(body, out_shape, operands, flops, in_specs=None, out_spec=VMEM, scratch=(), after=(), aliases=None):
    outs = jax.tree.leaves(out_shape)
    moved = sum(math.prod(a.shape) * a.dtype.itemsize for a in (*operands, *outs))
    read = len(operands)

    def whole(*refs):
        body(*refs[:read], *refs[read + len(after) :])

    return pl.pallas_call(
        whole,
        out_shape=out_shape,
        in_specs=[*(in_specs or [VMEM] * read), *[ANY] * len(after)],
        out_specs=jax.tree.map(lambda _: out_spec, out_shape),
        scratch_shapes=scratch,
        input_output_aliases=aliases or {},
        compiler_params=pltpu.CompilerParams(vmem_limit_bytes=24 << 20),
        cost_estimate=pl.CostEstimate(flops=flops, bytes_accessed=moved, transcendentals=0),
    )(*operands, *after)


def halves(x):
    high = x.astype(BF16)
    return high, (x - high.astype(F32)).astype(BF16)


def contract(first, second, dims):
    dot = functools.partial(
        lax.dot_general, dimension_numbers=(dims, ((), ())), preferred_element_type=F32
    )
    return dot(first[0], second[0]) + (dot(first[0], second[1]) + dot(first[1], second[0]))


def left(matrix, x):
    return contract((matrix[0], matrix[1]), halves(x), ((1,), (0,)))


def right(x, matrix):
    return contract(halves(x), (matrix[0], matrix[1]), ((1,), (0,)))


def order(gate, blocks):
    rows = lax.broadcasted_iota(jnp.int32, (gate, gate), 0)
    columns = lax.broadcasted_iota(jnp.int32, (gate, gate), 1)
    inside = columns % TILE
    middle = (columns // TILE) % blocks
    tile = columns // (TILE * blocks)
    return jnp.where(rows == (tile * TILE + inside) * blocks + middle, 1.0, 0.0).astype(BF16)


def exact(first, second, dims):
    return lax.dot_general(
        first, second, (dims, ((), ())), precision=lax.Precision.HIGHEST, preferred_element_type=F32
    )


def prepare_body(rounds, gate, blocks, gates_ref, *out_refs):
    permutation = order(gate, blocks).astype(F32)
    for number in range(rounds):
        for position in range(3):
            real = gates_ref[number, position, 0]
            imag = gates_ref[number, position, 1]
            if position == 2:
                real, imag = (
                    exact(exact(permutation, u, ((0,), (0,))), permutation, ((1,), (0,))) for u in (real, imag)
                )
            if position != 1:
                real, imag = real.T, imag.T
            for part, value in enumerate((real, imag)):
                for half, bits in enumerate(halves(value)):
                    out_refs[number][position, half, part] = bits


def united(gates_ref, position):
    for half in range(2):
        real, imag = gates_ref[position, half, 0], gates_ref[position, half, 1]
        above, below = (-imag, imag) if position == 1 else (imag, -imag)
        yield jnp.concatenate(
            [jnp.concatenate([real, above], axis=1), jnp.concatenate([below, real], axis=1)], axis=0
        )


def enter_body(gate, blocks, state_ref, adjoint_ref, out_ref, held_ref, tiles_ref, sems):
    size = 2 * blocks * TILE
    copies_in, copies_out = [], []
    for array, ref in enumerate((state_ref, adjoint_ref)):
        copies_in.append(pltpu.make_async_copy(ref, held_ref.at[array], sems.at[array]))
        at = pl.ds(array * size, size)
        copies_out.append(pltpu.make_async_copy(tiles_ref.at[:, at, :], out_ref.at[:, at, :], sems.at[2 + array]))
    for copy in copies_in:
        copy.start()
    for array in range(2):
        copies_in[array].wait()
        for part in range(2):
            for c in range(blocks):
                rows = held_ref[array, pl.ds(c * 2 + part, gate, stride=2 * blocks), :]
                at = ((array * 2 + part) * blocks + c) * TILE
                tiles_ref[:, pl.ds(at, TILE), :] = rows.reshape(gate // TILE, TILE, gate)
        copies_out[array].start()
    for copy in copies_out:
        copy.wait()


def last_input(x_ref, gate, blocks):
    tiles = gate // TILE // blocks
    size = blocks * TILE
    columns = []
    for array in range(2):
        for a1 in range(blocks):
            parts = [
                x_ref[pl.ds(a1 * tiles, tiles), pl.ds((array * 2 + part) * size, size), :].reshape(gate, gate)
                for part in range(2)
            ]
            columns.append(jnp.concatenate(parts, axis=0))
    return jnp.concatenate(columns, axis=1)


def middle_input(x, gate):
    rows = []
    for at in range(0, x.shape[1], gate):
        columns = x[:, at : at + gate]
        rows.append(jnp.concatenate([columns[:gate], columns[gate:]], axis=1))
    return jnp.concatenate(rows, axis=0)


def first_input(x, gate, blocks):
    columns = []
    for at in range(0, x.shape[0], blocks * gate):
        tiles = x[at : at + blocks * gate].reshape(gate // TILE, blocks, TILE, 2 * gate)
        for c in range(blocks):
            rows = tiles[:, c].reshape(gate, 2 * gate)
            columns.append(jnp.concatenate([rows[:, :gate], rows[:, gate:]], axis=0))
    return jnp.concatenate(columns, axis=1)


def undone(x_ref, gates_ref, gate, blocks):
    x = left(tuple(united(gates_ref, 2)), last_input(x_ref, gate, blocks))
    x = right(middle_input(x, gate), tuple(united(gates_ref, 1)))
    return left(tuple(united(gates_ref, 0)), first_input(x, gate, blocks))


def piece(x, gate, blocks, array, part, c):
    at = (array * blocks + c) * gate
    return x[part * gate : (part + 1) * gate, at : at + gate]


def undo_body(gate, blocks, x_ref, gates_ref, out_ref, tiles_ref, sems):
    x = undone(x_ref, gates_ref, gate, blocks)
    size = 2 * blocks * TILE
    copies = []
    for array in range(2):
        for part in range(2):
            for c in range(blocks):
                rows = piece(x, gate, blocks, array, part, c).reshape(gate // TILE, TILE, gate)
                tiles_ref[:, pl.ds(((array * 2 + part) * blocks + c) * TILE, TILE), :] = rows
        at = pl.ds(array * size, size)
        copies.append(pltpu.make_async_copy(tiles_ref.at[:, at, :], out_ref.at[:, at, :], sems.at[array]))
        copies[-1].start()
    for copy in copies:
        copy.wait()


def leave_body(gate, blocks, x_ref, gates_ref, state_ref, adjoint_ref, over_ref):
    x = undone(x_ref, gates_ref, gate, blocks)
    for array, ref in enumerate((state_ref, adjoint_ref)):
        for part in range(2):
            for c in range(blocks):
                ref[pl.ds(c * 2 + part, gate, stride=2 * blocks), :] = piece(x, gate, blocks, array, part, c)
    over_ref[...] = jnp.zeros_like(over_ref)


def pair(x, gate):
    real = x[:gate, :gate] + x[gate:, gate:]
    imag = x[gate:, :gate] - x[:gate, gate:]
    return real, imag


def gradient_body(gate, blocks, factor, depth, x_ref, gates_ref, bits_ref, own_ref, other_ref, all_ref):
    size = blocks * gate
    raw = last_input(x_ref, gate, blocks)
    x = left(tuple(united(gates_ref, 2)), raw)
    last = contract(halves(raw[:, size:]), halves(x[:, :size]), ((1,), (1,)))
    x = middle_input(x, gate)
    y = right(x, tuple(united(gates_ref, 1)))
    middle = contract(halves(x[size:]), halves(y[:size]), ((0,), (0,)))
    x = first_input(y, gate, blocks)
    first = contract(halves(x[:, size:]), halves(left(tuple(united(gates_ref, 0)), x[:, :size])), ((1,), (1,)))
    for position, grads in enumerate((first, middle)):
        for part, value in enumerate(pair(grads, gate)):
            all_ref[pl.ds((position * 2 + part) * gate, gate), :] = factor * value
    permutation = order(gate, blocks)
    last = halves(factor * jnp.concatenate(pair(last, gate), axis=0))
    dot = functools.partial(lax.dot_general, dimension_numbers=(((1,), (1,)), ((), ())), preferred_element_type=F32)
    last = dot(last[0], permutation) + dot(last[1], permutation)
    for part in range(2):
        for tile in range(gate // TILE // blocks):
            for c in range(blocks):
                at = part * gate + (tile * blocks + c) * TILE
                to = (4 + part) * gate + tile * TILE * blocks + c
                all_ref[pl.ds(to, TILE, stride=blocks), :] = last[at : at + TILE]
    for away, ref in enumerate((own_ref, other_ref)):
        for at, to, size in pieces(bits_ref, depth, away, all_ref.shape[0]):
            ref[pl.ds(at, size), :] = all_ref[pl.ds(to, size), :]


def pieces(bits_ref, depth, away, rows):
    size = rows >> depth
    for place in range(1 << (depth - 1)):
        at = bits_ref[0] ^ away
        for k in range(1, depth):
            at = 2 * at + (bits_ref[k] ^ (place >> (depth - 1 - k) & 1))
        yield place * size, pl.multiple_of(at * size, TILE), size


def place_body(groups, bits_ref, *refs):
    out_ref, sems = refs[-2:]
    copies = []
    for at, (rounds, depth) in enumerate(groups):
        for away in range(2):
            for start, to, size in pieces(bits_ref, depth, away, out_ref.shape[1]):
                for place, number in enumerate(rounds):
                    copies.append(
                        pltpu.make_async_copy(
                            refs[2 * at + away].at[pl.ds(start * len(rounds) + place * size, size), :],
                            out_ref.at[number, pl.ds(to, size), :],
                            sems.at[len(copies)],
                        )
                    )
    for copy in copies:
        copy.start()
    for copy in copies:
        copy.wait()


def add_body(first_ref, second_ref, out_ref):
    out_ref[...] = first_ref[...] + second_ref[...]


def add(first, second, *after):
    return call(add_body, jax.ShapeDtypeStruct(first.shape, F32), (first, second), 0, after=after)


def join_body(first_ref, second_ref, out_ref):
    size = first_ref.shape[0]
    out_ref[pl.ds(0, size), :] = first_ref[...]
    out_ref[pl.ds(size, size), :] = second_ref[...]


def join(first, second, *after):
    shape = jax.ShapeDtypeStruct((2 * first.shape[0], first.shape[1]), F32)
    return call(join_body, shape, (first, second), 0, after=after)


def exchange(x, shards, step):
    return lax.ppermute(x, "qa", [(i, i ^ step) for i in range(shards)])


def halved(total, shards, step):
    size = total.shape[0] // 2
    return total[:size] + exchange(total[size:], shards, step)


def doubled(total, shards, depth):
    for k in reversed(range(1, depth)):
        total = jnp.concatenate([total, exchange(total, shards, 1 << k)])
    return total, exchange(total, shards, 1)


def swapped(x, shards, gate):
    tiles, rows, _ = x.shape
    groups = rows // TILE
    if shards != tiles:
        x = x.reshape(tiles, groups, TILE, gate).swapaxes(0, 1).reshape(groups, shards, gate // shards, gate).swapaxes(0, 1)
    x = lax.all_to_all(x, "qa", split_axis=0, concat_axis=0, tiled=True)
    if shards != tiles:
        x = x.swapaxes(0, 1).reshape(groups, tiles, TILE, gate).swapaxes(0, 1).reshape(tiles, rows, gate)
    return x


def on_device(state, adjoint, gates):
    rounds, _, _, _, gate = gates.shape
    local_size = state.shape[1]
    shards = lax.axis_size("qa")
    index = lax.axis_index("qa")
    blocks = local_size // (gate * gate)
    factor = 1.0 / math.sqrt(shards * local_size // gate)
    tiles = gate // TILE
    rows = blocks * gate
    flat = jax.ShapeDtypeStruct((2 * rows, gate), F32)
    tiled = jax.ShapeDtypeStruct((tiles, 4 * blocks * TILE, gate), F32)
    work = 48 * local_size * gate

    matrices = call(
        functools.partial(prepare_body, rounds, gate, blocks),
        [jax.ShapeDtypeStruct((3, 2, 2, gate, gate), BF16)] * rounds,
        (gates,),
        rounds * 12 * 2 * gate**3,
    )
    steps = [1 << k for k in range(shards.bit_length() - 1)]
    early_depth, late_depth = DEPTHS
    stepwise = shards == 1 << len(steps) and len(steps) >= max(DEPTHS)
    bits = jnp.stack([index >> k & 1 if stepwise else index * 0 for k in range(max(DEPTHS))]).astype(jnp.int32)

    def entering(x):
        return x.reshape(2, rows, gate).swapaxes(0, 1).reshape(2 * rows, gate)

    def leaving(x):
        return x.reshape(rows, 2, gate).swapaxes(0, 1).reshape(2, local_size)

    x = call(
        functools.partial(enter_body, gate, blocks),
        tiled,
        [pltpu.with_memory_space_constraint(entering(array), pltpu.HBM) for array in (state, adjoint)],
        0,
        [ANY, ANY],
        ANY,
        [
            pltpu.VMEM((2, 2 * rows, gate), F32),
            pltpu.VMEM(tiled.shape, F32),
            pltpu.SemaphoreType.DMA((4,)),
        ],
    )
    totals, left_over, plain = [], [], []
    for number in reversed(range(rounds)):
        x = swapped(x, shards, gate)
        if number < rounds - 1:
            for at in range(len(totals)):
                if number == 0 or at < len(totals) - 1:
                    for step in left_over[at]:
                        totals[at] = halved(totals[at], shards, step)
                    left_over[at] = []
        own, other = call(
            functools.partial(gradient_body, gate, blocks, factor, early_depth if number > 0 else late_depth),
            [jax.ShapeDtypeStruct((3 * gate, gate), F32)] * 2,
            (x, matrices[number], bits),
            work,
            [VMEM, VMEM, SMEM],
            scratch=[pltpu.VMEM((6 * gate, gate), F32)],
            after=totals if number == 0 else (),
        )
        if stepwise:
            total = own + exchange(other, shards, steps[0])
        else:
            plain.append(lax.psum(jnp.concatenate([own, other]), "qa"))
        if number > 0:
            x = call(
                functools.partial(undo_body, gate, blocks),
                tiled,
                (x, matrices[number]),
                work,
                out_spec=ANY,
                scratch=[pltpu.VMEM(tiled.shape, F32), pltpu.SemaphoreType.DMA((2,))],
                after=totals,
            )
            if stepwise:
                totals.append(halved(total, shards, steps[1]))
                left_over.append(steps[2:early_depth])
    token = jax.ShapeDtypeStruct((TILE, gate), F32)
    state, adjoint, over = call(
        functools.partial(leave_body, gate, blocks), [flat, flat, token], (x, matrices[0]), work, after=totals
    )
    if not stepwise:
        return leaving(state), leaving(adjoint), jnp.stack(plain[::-1]).reshape(gates.shape)
    groups = (tuple(reversed(range(2, rounds))), (1,))
    early = []
    for group in groups:
        part = jnp.concatenate([totals[rounds - 1 - number] for number in group])
        for step in steps[early_depth:]:
            part = part + exchange(part, shards, step)
        early.append(doubled(part, shards, early_depth))
    late = total
    for step in steps[1:late_depth]:
        late = halved(late, shards, step)
    for step in steps[late_depth + 1 :]:
        late = late + exchange(late, shards, step)
    late = add(late, exchange(late, shards, steps[late_depth]), over)
    finished = [*early, doubled(late, shards, late_depth)]
    placed = jax.ShapeDtypeStruct((rounds, 6 * gate, gate), F32)
    first = [half for pair_of in finished[:-1] for half in pair_of]
    grads = call(
        functools.partial(place_body, tuple((group, early_depth) for group in groups)),
        placed,
        (bits, *first),
        0,
        [SMEM] + [ANY] * len(first),
        ANY,
        [pltpu.SemaphoreType.DMA((rounds << early_depth,))],
    )
    grads = call(
        functools.partial(place_body, (((0,), late_depth),)),
        placed,
        (bits, *finished[-1], grads),
        0,
        [SMEM] + [ANY] * 3,
        ANY,
        [pltpu.SemaphoreType.DMA((1 << late_depth,))],
        aliases={3: 0},
    )
    return leaving(state), leaving(adjoint), grads.reshape(gates.shape)


def solution(mesh):
    return jax.shard_map(
        on_device,
        mesh=mesh,
        in_specs=(P(None, ("grp", "qa")), P(None, ("grp", "qa")), P("grp", None, None, None, None)),
        out_specs=(
            P(None, ("grp", "qa")),
            P(None, ("grp", "qa")),
            P("grp", None, None, None, None),
        ),
        check_vma=False,
    )
```

```python
import functools
import math

import jax
import jax.numpy as jnp
from jax import lax
from jax.experimental import pallas as pl
from jax.experimental.pallas import tpu as pltpu
from jax.sharding import PartitionSpec as P

TILE = 8
VMEM = pl.BlockSpec(memory_space=pltpu.VMEM)
ANY = pl.BlockSpec(memory_space=pl.ANY)
SMEM = pl.BlockSpec(memory_space=pltpu.SMEM)
DEPTHS = (3, 2)
F32 = jnp.float32
BF16 = jnp.bfloat16


def call(body, out_shape, operands, flops, in_specs=None, out_spec=VMEM, scratch=(), after=(), aliases=None):
    outs = jax.tree.leaves(out_shape)
    moved = sum(math.prod(a.shape) * a.dtype.itemsize for a in (*operands, *outs))
    read = len(operands)

    def whole(*refs):
        body(*refs[:read], *refs[read + len(after) :])

    return pl.pallas_call(
        whole,
        out_shape=out_shape,
        in_specs=[*(in_specs or [VMEM] * read), *[ANY] * len(after)],
        out_specs=jax.tree.map(lambda _: out_spec, out_shape),
        scratch_shapes=scratch,
        input_output_aliases=aliases or {},
        compiler_params=pltpu.CompilerParams(vmem_limit_bytes=24 << 20),
        cost_estimate=pl.CostEstimate(flops=flops, bytes_accessed=moved, transcendentals=0),
    )(*operands, *after)


def halves(x):
    high = x.astype(BF16)
    return high, (x - high.astype(F32)).astype(BF16)


def contract(first, second, dims):
    dot = functools.partial(
        lax.dot_general, dimension_numbers=(dims, ((), ())), preferred_element_type=F32
    )
    return dot(first[0], second[0]) + (dot(first[0], second[1]) + dot(first[1], second[0]))


def left(matrix, x):
    return contract((matrix[0], matrix[1]), halves(x), ((1,), (0,)))


def right(x, matrix):
    return contract(halves(x), (matrix[0], matrix[1]), ((1,), (0,)))


def order(gate, blocks):
    rows = lax.broadcasted_iota(jnp.int32, (gate, gate), 0)
    columns = lax.broadcasted_iota(jnp.int32, (gate, gate), 1)
    inside = columns % TILE
    middle = (columns // TILE) % blocks
    tile = columns // (TILE * blocks)
    return jnp.where(rows == (tile * TILE + inside) * blocks + middle, 1.0, 0.0).astype(BF16)


def exact(first, second, dims):
    return lax.dot_general(
        first, second, (dims, ((), ())), precision=lax.Precision.HIGHEST, preferred_element_type=F32
    )


def prepare_body(rounds, gate, blocks, gates_ref, *out_refs):
    permutation = order(gate, blocks).astype(F32)
    for number in range(rounds):
        for position in range(3):
            real = gates_ref[number, position, 0]
            imag = gates_ref[number, position, 1]
            if position == 2:
                real, imag = (
                    exact(exact(permutation, u, ((0,), (0,))), permutation, ((1,), (0,))) for u in (real, imag)
                )
            if position != 1:
                real, imag = real.T, imag.T
            for part, value in enumerate((real, imag)):
                for half, bits in enumerate(halves(value)):
                    out_refs[number][position, half, part] = bits


def united(gates_ref, position):
    for half in range(2):
        real, imag = gates_ref[position, half, 0], gates_ref[position, half, 1]
        above, below = (-imag, imag) if position == 1 else (imag, -imag)
        yield jnp.concatenate(
            [jnp.concatenate([real, above], axis=1), jnp.concatenate([below, real], axis=1)], axis=0
        )


def enter_body(gate, blocks, state_ref, adjoint_ref, out_ref, held_ref, tiles_ref, sems):
    size = 2 * blocks * TILE
    copies_in, copies_out = [], []
    for array, ref in enumerate((state_ref, adjoint_ref)):
        copies_in.append(pltpu.make_async_copy(ref, held_ref.at[array], sems.at[array]))
        at = pl.ds(array * size, size)
        copies_out.append(pltpu.make_async_copy(tiles_ref.at[:, at, :], out_ref.at[:, at, :], sems.at[2 + array]))
    for copy in copies_in:
        copy.start()
    for array in range(2):
        copies_in[array].wait()
        for part in range(2):
            for c in range(blocks):
                rows = held_ref[array, pl.ds(c * 2 + part, gate, stride=2 * blocks), :]
                at = ((array * 2 + part) * blocks + c) * TILE
                tiles_ref[:, pl.ds(at, TILE), :] = rows.reshape(gate // TILE, TILE, gate)
        copies_out[array].start()
    for copy in copies_out:
        copy.wait()


def last_input(x_ref, gate, blocks):
    tiles = gate // TILE // blocks
    size = blocks * TILE
    columns = []
    for array in range(2):
        for a1 in range(blocks):
            parts = [
                x_ref[pl.ds(a1 * tiles, tiles), pl.ds((array * 2 + part) * size, size), :].reshape(gate, gate)
                for part in range(2)
            ]
            columns.append(jnp.concatenate(parts, axis=0))
    return jnp.concatenate(columns, axis=1)


def middle_input(x, gate):
    rows = []
    for at in range(0, x.shape[1], gate):
        columns = x[:, at : at + gate]
        rows.append(jnp.concatenate([columns[:gate], columns[gate:]], axis=1))
    return jnp.concatenate(rows, axis=0)


def first_input(x, gate, blocks):
    columns = []
    for at in range(0, x.shape[0], blocks * gate):
        tiles = x[at : at + blocks * gate].reshape(gate // TILE, blocks, TILE, 2 * gate)
        for c in range(blocks):
            rows = tiles[:, c].reshape(gate, 2 * gate)
            columns.append(jnp.concatenate([rows[:, :gate], rows[:, gate:]], axis=0))
    return jnp.concatenate(columns, axis=1)


def undone(x_ref, gates_ref, gate, blocks):
    x = left(tuple(united(gates_ref, 2)), last_input(x_ref, gate, blocks))
    x = right(middle_input(x, gate), tuple(united(gates_ref, 1)))
    return left(tuple(united(gates_ref, 0)), first_input(x, gate, blocks))


def piece(x, gate, blocks, array, part, c):
    at = (array * blocks + c) * gate
    return x[part * gate : (part + 1) * gate, at : at + gate]


def undo_body(gate, blocks, x_ref, gates_ref, out_ref, tiles_ref, sems):
    x = undone(x_ref, gates_ref, gate, blocks)
    size = 2 * blocks * TILE
    copies = []
    for array in range(2):
        for part in range(2):
            for c in range(blocks):
                rows = piece(x, gate, blocks, array, part, c).reshape(gate // TILE, TILE, gate)
                tiles_ref[:, pl.ds(((array * 2 + part) * blocks + c) * TILE, TILE), :] = rows
        at = pl.ds(array * size, size)
        copies.append(pltpu.make_async_copy(tiles_ref.at[:, at, :], out_ref.at[:, at, :], sems.at[array]))
        copies[-1].start()
    for copy in copies:
        copy.wait()


def leave_body(gate, blocks, x_ref, gates_ref, state_ref, adjoint_ref, over_ref):
    x = undone(x_ref, gates_ref, gate, blocks)
    for array, ref in enumerate((state_ref, adjoint_ref)):
        for part in range(2):
            for c in range(blocks):
                ref[pl.ds(c * 2 + part, gate, stride=2 * blocks), :] = piece(x, gate, blocks, array, part, c)
    over_ref[...] = jnp.zeros_like(over_ref)


def pair(x, gate):
    real = x[:gate, :gate] + x[gate:, gate:]
    imag = x[gate:, :gate] - x[:gate, gate:]
    return real, imag


def gradient_body(gate, blocks, factor, depth, x_ref, gates_ref, bits_ref, own_ref, other_ref, all_ref):
    size = blocks * gate
    raw = last_input(x_ref, gate, blocks)
    x = left(tuple(united(gates_ref, 2)), raw)
    last = contract(halves(raw[:, size:]), halves(x[:, :size]), ((1,), (1,)))
    x = middle_input(x, gate)
    y = right(x, tuple(united(gates_ref, 1)))
    middle = contract(halves(x[size:]), halves(y[:size]), ((0,), (0,)))
    x = first_input(y, gate, blocks)
    first = contract(halves(x[:, size:]), halves(left(tuple(united(gates_ref, 0)), x[:, :size])), ((1,), (1,)))
    for position, grads in enumerate((first, middle)):
        for part, value in enumerate(pair(grads, gate)):
            all_ref[pl.ds((position * 2 + part) * gate, gate), :] = factor * value
    permutation = order(gate, blocks)
    last = halves(factor * jnp.concatenate(pair(last, gate), axis=0))
    dot = functools.partial(lax.dot_general, dimension_numbers=(((1,), (1,)), ((), ())), preferred_element_type=F32)
    last = dot(last[0], permutation) + dot(last[1], permutation)
    for part in range(2):
        for tile in range(gate // TILE // blocks):
            for c in range(blocks):
                at = part * gate + (tile * blocks + c) * TILE
                to = (4 + part) * gate + tile * TILE * blocks + c
                all_ref[pl.ds(to, TILE, stride=blocks), :] = last[at : at + TILE]
    for away, ref in enumerate((own_ref, other_ref)):
        for at, to, size in pieces(bits_ref, depth, away, all_ref.shape[0]):
            ref[pl.ds(at, size), :] = all_ref[pl.ds(to, size), :]


def pieces(bits_ref, depth, away, rows):
    size = rows >> depth
    for place in range(1 << (depth - 1)):
        at = bits_ref[0] ^ away
        for k in range(1, depth):
            at = 2 * at + (bits_ref[k] ^ (place >> (depth - 1 - k) & 1))
        yield place * size, pl.multiple_of(at * size, TILE), size


def place_body(groups, bits_ref, *refs):
    out_ref, sems = refs[-2:]
    copies = []
    for at, (rounds, depth) in enumerate(groups):
        for away in range(2):
            for start, to, size in pieces(bits_ref, depth, away, out_ref.shape[1]):
                for place, number in enumerate(rounds):
                    copies.append(
                        pltpu.make_async_copy(
                            refs[2 * at + away].at[pl.ds(start * len(rounds) + place * size, size), :],
                            out_ref.at[number, pl.ds(to, size), :],
                            sems.at[len(copies)],
                        )
                    )
    for copy in copies:
        copy.start()
    for copy in copies:
        copy.wait()


def add_body(first_ref, second_ref, out_ref):
    out_ref[...] = first_ref[...] + second_ref[...]


def add(first, second, *after):
    return call(add_body, jax.ShapeDtypeStruct(first.shape, F32), (first, second), 0, after=after)


def join_body(first_ref, second_ref, out_ref):
    size = first_ref.shape[0]
    out_ref[pl.ds(0, size), :] = first_ref[...]
    out_ref[pl.ds(size, size), :] = second_ref[...]


def join(first, second, *after):
    shape = jax.ShapeDtypeStruct((2 * first.shape[0], first.shape[1]), F32)
    return call(join_body, shape, (first, second), 0, after=after)


def exchange(x, shards, step):
    return lax.ppermute(x, "qa", [(i, i ^ step) for i in range(shards)])


def halved(total, shards, step):
    size = total.shape[0] // 2
    return total[:size] + exchange(total[size:], shards, step)


def doubled(total, shards, depth):
    for k in reversed(range(1, depth)):
        total = jnp.concatenate([total, exchange(total, shards, 1 << k)])
    return total, exchange(total, shards, 1)


def swapped(x, shards, gate):
    tiles, rows, _ = x.shape
    groups = rows // TILE
    if shards != tiles:
        x = x.reshape(tiles, groups, TILE, gate).swapaxes(0, 1).reshape(groups, shards, gate // shards, gate).swapaxes(0, 1)
    x = lax.all_to_all(x, "qa", split_axis=0, concat_axis=0, tiled=True)
    if shards != tiles:
        x = x.swapaxes(0, 1).reshape(groups, tiles, TILE, gate).swapaxes(0, 1).reshape(tiles, rows, gate)
    return x


def on_device(state, adjoint, gates):
    rounds, _, _, _, gate = gates.shape
    local_size = state.shape[1]
    shards = lax.axis_size("qa")
    index = lax.axis_index("qa")
    blocks = local_size // (gate * gate)
    factor = 1.0 / math.sqrt(shards * local_size // gate)
    tiles = gate // TILE
    rows = blocks * gate
    flat = jax.ShapeDtypeStruct((2 * rows, gate), F32)
    tiled = jax.ShapeDtypeStruct((tiles, 4 * blocks * TILE, gate), F32)
    work = 72 * local_size * gate

    matrices = call(
        functools.partial(prepare_body, rounds, gate, blocks),
        [jax.ShapeDtypeStruct((3, 2, 2, gate, gate), BF16)] * rounds,
        (gates,),
        rounds * 12 * 2 * gate**3,
    )
    steps = [1 << k for k in range(shards.bit_length() - 1)]
    early_depth, late_depth = DEPTHS
    stepwise = shards == 1 << len(steps) and len(steps) >= max(DEPTHS)
    bits = jnp.stack([index >> k & 1 if stepwise else index * 0 for k in range(max(DEPTHS))]).astype(jnp.int32)

    def entering(x):
        return x.reshape(2, rows, gate).swapaxes(0, 1).reshape(2 * rows, gate)

    def leaving(x):
        return x.reshape(rows, 2, gate).swapaxes(0, 1).reshape(2, local_size)

    x = call(
        functools.partial(enter_body, gate, blocks),
        tiled,
        [pltpu.with_memory_space_constraint(entering(array), pltpu.HBM) for array in (state, adjoint)],
        0,
        [ANY, ANY],
        ANY,
        [
            pltpu.VMEM((2, 2 * rows, gate), F32),
            pltpu.VMEM(tiled.shape, F32),
            pltpu.SemaphoreType.DMA((4,)),
        ],
    )
    totals, left_over, plain = [], [], []
    for number in reversed(range(rounds)):
        x = swapped(x, shards, gate)
        if number < rounds - 1:
            for at in range(len(totals)):
                if number == 0 or at < len(totals) - 1:
                    for step in left_over[at]:
                        totals[at] = halved(totals[at], shards, step)
                    left_over[at] = []
        own, other = call(
            functools.partial(gradient_body, gate, blocks, factor, early_depth if number > 0 else late_depth),
            [jax.ShapeDtypeStruct((3 * gate, gate), F32)] * 2,
            (x, matrices[number], bits),
            0,
            [VMEM, VMEM, SMEM],
            scratch=[pltpu.VMEM((6 * gate, gate), F32)],
            after=totals if number == 0 else (),
        )
        if stepwise:
            total = own + exchange(other, shards, steps[0])
        else:
            plain.append(lax.psum(jnp.concatenate([own, other]), "qa"))
        if number > 0:
            x = call(
                functools.partial(undo_body, gate, blocks),
                tiled,
                (x, matrices[number]),
                0,
                out_spec=ANY,
                scratch=[pltpu.VMEM(tiled.shape, F32), pltpu.SemaphoreType.DMA((2,))],
                after=totals,
            )
            if stepwise:
                totals.append(halved(total, shards, steps[1]))
                left_over.append(steps[2:early_depth])
    token = jax.ShapeDtypeStruct((TILE, gate), F32)
    state, adjoint, over = call(
        functools.partial(leave_body, gate, blocks), [flat, flat, token], (x, matrices[0]), work, after=totals
    )
    if not stepwise:
        return leaving(state), leaving(adjoint), jnp.stack(plain[::-1]).reshape(gates.shape)
    groups = (tuple(reversed(range(2, rounds))), (1,))
    early = []
    for group in groups:
        part = jnp.concatenate([totals[rounds - 1 - number] for number in group])
        for step in steps[early_depth:]:
            part = part + exchange(part, shards, step)
        early.append(doubled(part, shards, early_depth))
    late = total
    for step in steps[1:late_depth]:
        late = halved(late, shards, step)
    for step in steps[late_depth + 1 :]:
        late = late + exchange(late, shards, step)
    late = add(late, exchange(late, shards, steps[late_depth]), over)
    finished = [*early, doubled(late, shards, late_depth)]
    placed = jax.ShapeDtypeStruct((rounds, 6 * gate, gate), F32)
    first = [half for pair_of in finished[:-1] for half in pair_of]
    grads = call(
        functools.partial(place_body, tuple((group, early_depth) for group in groups)),
        placed,
        (bits, *first),
        0,
        [SMEM] + [ANY] * len(first),
        ANY,
        [pltpu.SemaphoreType.DMA((rounds << early_depth,))],
    )
    grads = call(
        functools.partial(place_body, (((0,), late_depth),)),
        placed,
        (bits, *finished[-1], grads),
        0,
        [SMEM] + [ANY] * 3,
        ANY,
        [pltpu.SemaphoreType.DMA((1 << late_depth,))],
        aliases={3: 0},
    )
    return leaving(state), leaving(adjoint), grads.reshape(gates.shape)


def solution(mesh):
    return jax.shard_map(
        on_device,
        mesh=mesh,
        in_specs=(P(None, ("grp", "qa")), P(None, ("grp", "qa")), P("grp", None, None, None, None)),
        out_specs=(
            P(None, ("grp", "qa")),
            P(None, ("grp", "qa")),
            P("grp", None, None, None, None),
        ),
        check_vma=False,
    )
```
